256 devices in a mesh: dp: 4 (over z_lo), sp: 64 (over x, z_hi, y, core).
Axes of the slice: x: 4, y: 4, z: 8 (z_hi: 2, z_lo: 4; z = z_hi * 4 + z_lo), core: 2. Of those that a mesh axis runs over, the one named last changes fastest.
Arguments:
- inputs: bfloat16 [4, 384, 768, 384], P('dp', 'sp'), may hold values from -6 to 6
- cotangent: bfloat16 [4, 384, 768, 384], P('dp', 'sp'), may hold values from -6 to 6
- masks: int32 [4, 256, 256, 384], P('dp', None, 'sp'), may hold values from 0 to 15
- w_first: bfloat16 [2, 4, 96, 96], replicated, may hold values from -0.4375 to 0.4375
- b_first: float32 [2, 384], replicated, may hold values from -4 to 4
- w_second: bfloat16 [2, 4, 96, 96], replicated, may hold values from -0.4375 to 0.4375
Outputs:
- grad_input: bfloat16 [4, 384, 768, 384], P('dp', 'sp')
- grad_w1: float32 [2, 4, 96, 96], replicated
- grad_b1: float32 [2, 384], replicated
- grad_w2: float32 [2, 4, 96, 96], replicated
- grad_b2: float32 [2, 384], replicated
The draws below stay inside these ranges and needn't reach their ends.
All inputs are finite; a program needn't handle non-finite values.
Results may differ from the reference program's by a relative error of at most 0.0086.
Values may be sent and summed in bfloat16 or wider, within the bound.
A program may use at most 128 MiB of HBM per device.

```python
import math
import jax
import jax.numpy as jnp
from jax import lax

LAT = 384
LON = 768
EMBED = 384
BLOCK = 96
NBLK = 4
KX = 256
KY = 256
MEMBERS = 4


def place_ends(array, rng, least, largest):
    place = [jax.random.randint(jax.random.fold_in(rng, axis), (), 0, length) for axis, length in enumerate(array.shape)]
    main_axis = array.shape.index(max(array.shape))
    neighbour = place[:main_axis] + [(place[main_axis] + 1) % array.shape[main_axis]] + place[main_axis + 1:]
    return array.at[tuple(place)].set(least).at[tuple(neighbour)].set(largest)


def level_of(own_key, extent, pieces, low, high):
    def one(axis_at, shards_of):
        heights = jax.random.uniform(jax.random.fold_in(jax.random.fold_in(own_key, 6), axis_at), (shards_of,), jnp.float32, low / len(pieces), high / len(pieces))
        return jnp.repeat(jnp.exp(heights), extent[axis_at] // shards_of).reshape((-1,) + (1,) * (len(extent) - axis_at - 1))

    factor_of = one(*pieces[0])
    for cut in pieces[1:]:
        factor_of = factor_of * one(*cut)
    return factor_of


def bell_draw(key, dims, spread, reach, pieces=(), held_as=jnp.bfloat16):
    array = spread * jax.random.normal(key, dims, jnp.float32)
    if pieces:
        array = array * level_of(key, dims, pieces, -0.22, 0.18)
    return jnp.clip(array, -reach, reach).astype(held_as)


def setup_inputs(seed: int = 0) -> dict:
    streams_of = jax.random.split(jax.random.key(seed), 7)
    return {
        "inputs": bell_draw(streams_of[0], (MEMBERS, LAT, LON, EMBED), 1.0, 6.0, ((0, 4), (1, 64))),
        "cotangent": bell_draw(streams_of[1], (MEMBERS, LAT, LON, EMBED), 1.0, 6.0, ((0, 4), (1, 64))),
        "masks": place_ends(jax.random.randint(streams_of[2], (MEMBERS, KY, KX, EMBED), 0, 16), jax.random.fold_in(streams_of[2], 1), 0, 15).astype(jnp.int32),
        "w_first": bell_draw(streams_of[3], (2, NBLK, BLOCK, BLOCK), (2 * BLOCK) ** -0.5, 0.4375),
        "b_first": bell_draw(streams_of[4], (2, EMBED), 1.0, 4.0, (), jnp.float32),
        "w_second": bell_draw(streams_of[5], (2, NBLK, BLOCK, BLOCK), (2 * BLOCK) ** -0.5, 0.4375),
    }


def lon_table(count, length):
    modes = jnp.arange(count, dtype=jnp.int32)
    points = jnp.arange(length, dtype=jnp.int32)
    phase = modes[:, None] * points[None, :] % length
    angle = 2.0 * math.pi / length * phase.astype(jnp.float32)
    return jnp.stack([jnp.cos(angle).astype(jnp.bfloat16), -jnp.sin(angle).astype(jnp.bfloat16)])

def lat_tables(keep, length):
    half_keep = keep // 2
    index = jnp.arange(keep, dtype=jnp.int32)
    modes = jnp.where(index < half_keep, index, index + (length - keep))
    points = jnp.arange(length, dtype=jnp.int32)
    phase = modes[:, None] * points[None, :] % length
    angle = 2.0 * math.pi / length * phase.astype(jnp.float32)
    cosine = jnp.cos(angle).astype(jnp.bfloat16)
    sine = jnp.sin(angle).astype(jnp.bfloat16)
    forward = jnp.stack([jnp.stack([cosine, sine], 1), jnp.stack([-sine, cosine], 1)])
    backward = jnp.stack([jnp.stack([cosine.T, -sine.T], 1), jnp.stack([sine.T, cosine.T], 1)])
    return (forward, backward)

def contract(form, left, right):
    return jnp.einsum(form, left.astype(jnp.float32), right.astype(jnp.float32), precision=lax.Precision.HIGHEST)

def complex_mul(real, imag, w_real, w_imag):
    form = 'jkbi,bio->jkbo'
    return (contract(form, real, w_real) - contract(form, imag, w_imag), contract(form, real, w_imag) + contract(form, imag, w_real))

def complex_adjoint(real, imag, w_real, w_imag):
    form = 'jkbo,bio->jkbi'
    return (contract(form, real, w_real) + contract(form, imag, w_imag), contract(form, imag, w_real) - contract(form, real, w_imag))

def weight_grad(left_re, left_im, right_re, right_im):
    form = 'jkbi,jkbo->bio'
    return jnp.stack([contract(form, left_re, right_re) + contract(form, left_im, right_im), contract(form, left_re, right_im) - contract(form, left_im, right_re)])

def bias_grad(real, imag):
    return jnp.stack([lax.optimization_barrier(jnp.sum(real.astype(jnp.float32), axis=(0, 1))), lax.optimization_barrier(jnp.sum(imag.astype(jnp.float32), axis=(0, 1)))]).reshape(2, EMBED)

def reference(inputs, cotangent, masks, w_first, b_first, w_second):
    lon_tab = lon_table(KX, LON)
    lat_fwd, lat_back = lat_tables(KY, LAT)
    factor = 1.0 / math.sqrt(LAT * LON)
    mode_weight = jnp.where(jnp.arange(KX) == 0, 1.0, 2.0).astype(jnp.float32)
    blocks = (KY, KX, NBLK, BLOCK)
    bias_re = b_first[0].reshape(NBLK, BLOCK)
    bias_im = b_first[1].reshape(NBLK, BLOCK)

    def member(carry, item):
        field, cotan, packed = item
        y_input = contract('pkw,hwc->pkhc', lon_tab, field).astype(jnp.bfloat16)
        y_cotan = contract('pkw,hwc->pkhc', lon_tab, cotan).astype(jnp.bfloat16)
        spectrum = (contract('qjph,pkhc->qjkc', lat_fwd, y_input) * factor).astype(jnp.bfloat16)
        d_out = (contract('qjph,pkhc->qjkc', lat_fwd, y_cotan) * factor * mode_weight[None, None, :, None]).astype(jnp.bfloat16)
        relu_re = (packed % 2).astype(jnp.float32).reshape(blocks)
        relu_im = (packed // 2 % 2).astype(jnp.float32).reshape(blocks)
        shrink_re = (packed // 4 % 2).astype(jnp.float32).reshape(blocks)
        shrink_im = (packed // 8 % 2).astype(jnp.float32).reshape(blocks)
        spec_re = spectrum[0].reshape(blocks)
        spec_im = spectrum[1].reshape(blocks)
        pre_re, pre_im = complex_mul(spec_re, spec_im, w_first[0], w_first[1])
        hidden_re = ((pre_re + bias_re) * relu_re).astype(jnp.bfloat16)
        hidden_im = ((pre_im + bias_im) * relu_im).astype(jnp.bfloat16)
        dtwo_re = (d_out[0].reshape(blocks).astype(jnp.float32) * shrink_re).astype(jnp.bfloat16)
        dtwo_im = (d_out[1].reshape(blocks).astype(jnp.float32) * shrink_im).astype(jnp.bfloat16)
        back_re, back_im = complex_adjoint(dtwo_re, dtwo_im, w_second[0], w_second[1])
        done_re = (back_re * relu_re).astype(jnp.bfloat16)
        done_im = (back_im * relu_im).astype(jnp.bfloat16)
        dspec_re, dspec_im = complex_adjoint(done_re, done_im, w_first[0], w_first[1])
        d_spec = jnp.stack([dspec_re, dspec_im]).reshape(2, KY, KX, EMBED).astype(jnp.bfloat16)
        image = contract('phqj,qjkc->phkc', lat_back, d_spec).astype(jnp.bfloat16)
        grad_field = (cotan.astype(jnp.float32) + factor * contract('pkw,phkc->hwc', lon_tab, image)).astype(jnp.bfloat16)
        terms = (weight_grad(spec_re, spec_im, done_re, done_im), bias_grad(done_re, done_im), weight_grad(hidden_re, hidden_im, dtwo_re, dtwo_im), bias_grad(dtwo_re, dtwo_im))
        return (tuple((total + term for total, term in zip(carry, terms))), grad_field)
    zero_w = jnp.zeros((2, NBLK, BLOCK, BLOCK), jnp.float32)
    zero_b = jnp.zeros((2, EMBED), jnp.float32)
    totals, grad_input = lax.scan(member, (zero_w, zero_b, zero_w, zero_b), (inputs, cotangent, masks))
    norm = 1.0 / math.sqrt(MEMBERS * KY * KX)
    return (grad_input, totals[0] * norm, totals[1] * norm, totals[2] * norm, totals[3] * norm)
```

```python
import functools
import math

import jax
import jax.numpy as jnp
import ml_dtypes
import numpy as np
from jax import lax
from jax.experimental import pallas as pl
from jax.experimental.pallas import tpu as pltpu
from jax.sharding import PartitionSpec as P

MESH = pl.DeviceIdType.MESH
BF = jnp.bfloat16
F32 = jnp.float32
MIB = 2**20


def bf(array):
    return array.astype(np.float32).astype(ml_dtypes.bfloat16)


def lon_tables(count, length, devices):
    phase = (np.arange(count)[:, None] * np.arange(length)[None, :]) % length
    angle = (np.float32(2.0 * math.pi / length) * phase.astype(np.float32)).astype(np.float64)
    table = np.stack([np.cos(angle), -np.sin(angle)], 1).reshape(2 * count, length)
    return bf(table), bf(table.T)


def lat_tables(keep, length):
    index = np.arange(keep)
    modes = np.where(index < keep // 2, index, index + (length - keep))
    phase = (modes[:, None] * np.arange(length)[None, :]) % length
    angle = (np.float32(2.0 * math.pi / length) * phase.astype(np.float32)).astype(np.float64)
    cosine, sine = np.cos(angle), np.sin(angle)
    forward = np.stack([np.stack([cosine, sine], 2), np.stack([-sine, cosine], 2)])
    return bf(forward.reshape(2 * keep, 2 * length)), bf(forward.reshape(2 * keep, 2 * length).T)


def permutation(rows, modes):
    out = np.zeros((modes, rows, 2, rows, modes, 2), np.float32)
    for k in range(modes):
        for h in range(rows):
            for p in range(2):
                out[k, h, p, h, k, p] = 1.0
    size = modes * rows * 2
    out = out.reshape(size, size)
    return bf(out), bf(out.T)


def dot(left, right):
    return jnp.dot(left, right, preferred_element_type=F32)


def dot_tn(left, right):
    return lax.dot_general(left, right, (((0,), (0,)), ((), ())), preferred_element_type=F32)


def main_kernel(
    factor, norm,
    cot_hbm, inp_hbm, mask_hbm, lon_hbm, latf_hbm, latb_hbm, pf_ref, pb_ref, w1_ref, b1_ref, w2_ref,
    rows_out, grads_out,
    cot_v, inp_v, mask_v, lon_v, latf_v, latb_v,
    send_c, send_i, send_r, recv_c, recv_i, xt, spec, dtwo, done, hid, dsp, relu, shrink,
    m1, m2, m3, acc_a, acc_b, acc_s, fold, parts, gathered, plane, column, chunk, result,
    lsem, ssem, rsem,
):
    dp = lax.axis_index("dp")
    me = lax.axis_index("sp")
    x = me // 16
    z_hi = (me // 8) % 2
    low = me % 8
    p1 = x * 8 + low
    zi = z_hi * 4 + dp

    loads = [
        pltpu.make_async_copy(lon_hbm, lon_v, lsem.at[0]),
        pltpu.make_async_copy(cot_hbm.at[pl.ds(0, 2)], cot_v.at[pl.ds(0, 2)], lsem.at[1]),
        pltpu.make_async_copy(cot_hbm.at[pl.ds(2, 4)], cot_v.at[pl.ds(2, 4)], lsem.at[2]),
        pltpu.make_async_copy(inp_hbm, inp_v, lsem.at[3]),
        pltpu.make_async_copy(mask_hbm, mask_v, lsem.at[4]),
        pltpu.make_async_copy(latf_hbm, latf_v, lsem.at[5]),
        pltpu.make_async_copy(latb_hbm, latb_v, lsem.at[6]),
    ]
    for load in loads:
        load.start()

    barrier = pltpu.get_barrier_semaphore()

    def greet(o, carry):
        pl.semaphore_signal(barrier, inc=1, device_id=(dp, (me + o) % 64), device_id_type=MESH)
        return carry

    lax.fori_loop(1, 64, greet, 0)
    for o in range(1, 4):
        for zh in range(2):
            pl.semaphore_signal(
                barrier, inc=1, device_id=((dp + o) % 4, x * 16 + zh * 8 + low), device_id_type=MESH
            )

    def transform(field, send, hp):
        def part(m, carry):
            table = lon_v[pl.ds(pl.multiple_of(m * 128, 128), 128), :]
            first = dot(table, field[2 * hp]).reshape(16, 8, 384)
            second = dot(table, field[2 * hp + 1]).reshape(16, 8, 384)
            send[hp, pl.ds(m * 16, 16)] = jnp.concatenate([first, second], axis=1).astype(BF)
            return carry

        lax.fori_loop(0, 4, part, 0)

    def send_rows(send, recv, slot, hp):
        place = pl.ds(pl.multiple_of(me * 48 + hp * 16, 16), 16)
        recv[place, :] = send[hp, me]

        def one(o, carry):
            there = (me + o) % 64
            pltpu.make_async_remote_copy(
                src_ref=send.at[hp, there], dst_ref=recv.at[place], send_sem=ssem.at[slot],
                recv_sem=rsem.at[slot], device_id=(dp, there), device_id_type=MESH,
            ).start()
            return carry

        lax.fori_loop(1, 64, one, 0)

    loads[0].wait()
    loads[1].wait()
    transform(cot_v, send_c, 0)
    pl.semaphore_wait(barrier, 69)
    send_rows(send_c, recv_c, 0, 0)
    loads[2].wait()

    def cot_pair(hp, carry):
        transform(cot_v, send_c, hp)
        send_rows(send_c, recv_c, 0, hp)
        return carry

    lax.fori_loop(1, 3, cot_pair, 0)
    loads[3].wait()

    def inp_pair(hp, carry):
        transform(inp_v, send_i, hp)
        send_rows(send_i, recv_i, 1, hp)
        return carry

    lax.fori_loop(0, 3, inp_pair, 0)

    lane = lax.broadcasted_iota(jnp.int32, (96, 384), 1)
    row = lax.broadcasted_iota(jnp.int32, (96, 384), 0)
    for b in range(4):
        place = (lane == row + 96 * b).astype(BF)
        up = slice(96 * b, 96 * b + 96)
        dn = slice(384 + 96 * b, 384 + 96 * b + 96)
        w1r, w1i = w1_ref[0, b], w1_ref[1, b]
        w2r, w2i = w2_ref[0, b], w2_ref[1, b]
        real, imag = dot(w1r, place).astype(BF), dot(w1i, place).astype(BF)
        m1[up, 0:384] = real
        m1[up, 384:768] = imag
        m1[dn, 0:384] = -imag
        m1[dn, 384:768] = real
        for target, wr, wi in ((m2, w2r, w2i), (m3, w1r, w1i)):
            real, imag = dot_tn(wr, place).astype(BF), dot_tn(wi, place).astype(BF)
            target[up, 0:384] = real
            target[up, 384:768] = -imag
            target[dn, 0:384] = imag
            target[dn, 384:768] = real
    loads[4].wait()
    for kk in range(4):
        bits = mask_v[:, kk, :]
        here = slice(256 * kk, 256 * kk + 256)
        relu[here, 0:384] = (bits & 1).astype(F32).astype(BF)
        relu[here, 384:768] = ((bits >> 1) & 1).astype(F32).astype(BF)
        shrink[here, 0:384] = ((bits >> 2) & 1).astype(F32).astype(BF)
        shrink[here, 384:768] = ((bits >> 3) & 1).astype(F32).astype(BF)
    loads[5].wait()
    loads[6].wait()

    def arrived(recv, slot):
        view = recv.at[pl.ds(0, 63 * 48)]
        pltpu.make_async_remote_copy(
            src_ref=view, dst_ref=view, send_sem=ssem.at[slot], recv_sem=rsem.at[slot],
            device_id=(dp, me), device_id_type=MESH,
        ).wait_recv()

    def by_mode(recv):
        def block(g, carry):
            rows = dot(pf_ref[...], recv[pl.ds(pl.multiple_of(g * 256, 256), 256), :]).astype(BF)
            for kk in range(4):
                xt[kk, pl.ds(pl.multiple_of(g * 64, 64), 64), :] = rows[64 * kk:64 * kk + 64]
            return carry

        lax.fori_loop(0, 12, block, 0)

    def mode_rows(kk):
        return pl.ds(pl.multiple_of(kk * 256, 256), 256)

    arrived(recv_c, 0)
    by_mode(recv_c)

    def adjoint(kk, carry):
        here = mode_rows(kk)
        scale = jnp.where(me * 4 + kk == 0, factor, 2.0 * factor).astype(F32)
        for q in range(2):
            cols = slice(384 * q, 384 * q + 384)
            d_out = (dot(latf_v[256 * q:256 * q + 256, :], xt[kk]) * scale).astype(BF)
            dtwo[here, cols] = d_out * shrink[here, cols]
        back = dot(dtwo[here, :], m2[...]) * relu[here, :].astype(F32)
        done[here, :] = back.astype(BF)
        d_spec = dot(done[here, :], m3[...]).astype(BF)
        dsp[kk, 0:256, :] = d_spec[:, 0:384]
        dsp[kk, 256:512, :] = d_spec[:, 384:768]
        return carry

    lax.fori_loop(0, 4, adjoint, 0)

    own = pltpu.make_async_copy(
        send_r.at[pl.ds(pl.multiple_of(me * 48, 16), 48)],
        rows_out.at[pl.ds(pl.multiple_of(me * 48, 16), 48)], lsem.at[7],
    )

    def image_quarter(m):
        def block(b, carry):
            table = latb_v[pl.ds(pl.multiple_of(m * 192 + b * 64, 64), 64), :]
            image = jnp.concatenate([dot(table, dsp[kk]).astype(BF) for kk in range(4)], axis=0)
            place = pl.ds(pl.multiple_of(m * 768 + b * 256, 256), 256)
            send_r[place, :] = dot(pb_ref[...], image).astype(BF)
            return carry

        lax.fori_loop(0, 3, block, 0)

    for i in range(4):
        m = (x + i) % 4
        image_quarter(m)
        if i == 0:
            own.start()

        def one(o, carry):
            there = m * 16 + (me + o) % 16
            pltpu.make_async_remote_copy(
                src_ref=send_r.at[pl.ds(pl.multiple_of(there * 48, 16), 48)],
                dst_ref=rows_out.at[pl.ds(pl.multiple_of(me * 48, 16), 48)],
                send_sem=ssem.at[2], recv_sem=rsem.at[2],
                device_id=(dp, there), device_id_type=MESH,
            ).start()
            return carry

        lax.fori_loop(1 if i == 0 else 0, 16, one, 0)

    arrived(recv_i, 1)
    by_mode(recv_i)

    def layer(kk, carry):
        here = mode_rows(kk)
        for q in range(2):
            cols = slice(384 * q, 384 * q + 384)
            spec[here, cols] = (dot(latf_v[256 * q:256 * q + 256, :], xt[kk]) * factor).astype(BF)
        pre = dot(spec[here, :], m1[...])
        for q in range(2):
            cols = slice(384 * q, 384 * q + 384)
            kept = (pre[:, cols] + b1_ref[q:q + 1, :]) * relu[here, cols].astype(F32)
            hid[here, cols] = kept.astype(BF)
        return carry

    lax.fori_loop(0, 4, layer, 0)

    lanes = lax.broadcasted_iota(jnp.int32, (96, 384), 1) // 96
    for which, (left, right) in enumerate(((spec, done), (hid, dtwo))):
        acc_a[...] = jnp.zeros_like(acc_a)
        acc_b[...] = jnp.zeros_like(acc_b)
        acc_s[...] = jnp.zeros_like(acc_s)

        def add(kk, carry, left=left, right=right):
            here = mode_rows(kk)
            r = right[here, :]
            acc_a[...] += dot_tn(left[here, 0:384], r)
            acc_b[...] += dot_tn(left[here, 384:768], r)
            acc_s[...] += dot(jnp.ones((8, 256), BF), r)
            return carry

        lax.fori_loop(0, 4, add, 0)
        real = jnp.zeros((96, 384), F32)
        imag = jnp.zeros((96, 384), F32)
        for b in range(4):
            up = slice(96 * b, 96 * b + 96)
            real = jnp.where(lanes == b, acc_a[up, 0:384] + acc_b[up, 384:768], real)
            imag = jnp.where(lanes == b, acc_a[up, 384:768] - acc_b[up, 0:384], imag)
        fold[0:96, 0:384] = real
        fold[0:96, 384:768] = imag
        for r in range(12):
            for c in range(6):
                t = which * 72 + r * 6 + c
                parts[t // 5, t % 5] = fold[8 * r:8 * r + 8, 128 * c:128 * c + 128]
        for c in range(6):
            t = 144 + c
            sums = acc_s[:, 128 * c:128 * c + 128]
            if which == 0:
                parts[t // 5, t % 5] = sums
            else:
                first = lax.broadcasted_iota(jnp.int32, (8, 128), 0) == 0
                parts[t // 5, t % 5] = jnp.where(first, parts[t // 5, t % 5], sums)
    for t in range(150, 160):
        parts[t // 5, t % 5] = jnp.zeros((8, 128), F32)

    def in_plane(p):
        return (p // 8) * 16 + z_hi * 8 + p % 8

    def wait_all(ref, count, slot):
        view = ref.at[pl.ds(0, count)]
        pltpu.make_async_remote_copy(
            src_ref=view, dst_ref=view, send_sem=ssem.at[slot], recv_sem=rsem.at[slot],
            device_id=(dp, me), device_id_type=MESH,
        ).wait()

    plane[p1] = parts[p1]

    def scatter(o, carry):
        p = (p1 + o) % 32
        pltpu.make_async_remote_copy(
            src_ref=parts.at[p], dst_ref=plane.at[p1], send_sem=ssem.at[3], recv_sem=rsem.at[3],
            device_id=(dp, in_plane(p)), device_id_type=MESH,
        ).start()
        return carry

    lax.fori_loop(1, 32, scatter, 0)
    wait_all(plane, 31, 3)
    chunk[...] = plane[0]

    def add_plane(p, carry):
        chunk[...] += plane[p]
        return carry

    lax.fori_loop(1, 32, add_plane, 0)
    column[zi] = chunk[...]

    def along_z(o, carry):
        z = (zi + o) % 8
        pltpu.make_async_remote_copy(
            src_ref=chunk, dst_ref=column.at[zi], send_sem=ssem.at[4], recv_sem=rsem.at[4],
            device_id=(z % 4, x * 16 + (z // 4) * 8 + low), device_id_type=MESH,
        ).start()
        return carry

    lax.fori_loop(1, 8, along_z, 0)
    wait_all(column, 7, 4)
    total = column[0]
    for z in range(1, 8):
        total = total + column[z]
    result[...] = total * norm
    gathered[p1] = result[...]

    def gather(o, carry):
        p = (p1 + o) % 32
        pltpu.make_async_remote_copy(
            src_ref=result, dst_ref=gathered.at[p1], send_sem=ssem.at[5], recv_sem=rsem.at[5],
            device_id=(dp, in_plane(p)), device_id_type=MESH,
        ).start()
        return carry

    lax.fori_loop(1, 32, gather, 0)
    wait_all(gathered, 31, 5)
    grads_out[...] = gathered[...]

    own.wait()
    arrived(rows_out, 2)
    for slot in range(3):
        view = recv_c.at[pl.ds(0, 63 * 48)]
        pltpu.make_async_remote_copy(
            src_ref=view, dst_ref=view, send_sem=ssem.at[slot], recv_sem=rsem.at[slot],
            device_id=(dp, me), device_id_type=MESH,
        ).wait_send()


def last_kernel(factor, rows_ref, cot_ref, table_ref, grads_ref, out_ref, w1_out, b1_out, w2_out, b2_out):
    rows = rows_ref[:, 0].astype(F32)
    for half in range(2):
        image = rows[:, 8 * half:8 * half + 8, :].reshape(512, 384).astype(BF)
        for m in range(3):
            part = slice(256 * m, 256 * m + 256)
            field = dot(table_ref[part, :], image) * factor
            out_ref[half, part, :] = (cot_ref[half, part, :].astype(F32) + field).astype(BF)

    @pl.when(pl.program_id(0) == 0)
    def _():
        def tiles(first):
            return jnp.concatenate(
                [grads_ref[t // 5, t % 5] for t in range(first, first + 6)], axis=1
            )

        for which, out in enumerate((w1_out, w2_out)):
            for r in range(12):
                line = tiles(which * 72 + r * 6)
                for q in range(2):
                    for b in range(4):
                        start = q * 384 + b * 96
                        out[q, b, 8 * r:8 * r + 8, :] = line[:, start:start + 96]
        line = tiles(144)
        for which, out in enumerate((b1_out, b2_out)):
            for q in range(2):
                out[q:q + 1, :] = line[which:which + 1, 384 * q:384 * q + 384]


def local(inputs, cotangent, masks, w_first, b_first, w_second):
    factor = 1.0 / math.sqrt(384 * 768)
    norm = 1.0 / math.sqrt(4 * 256 * 256)
    lon, lon_t = lon_tables(256, 768, 64)
    lat_f, lat_b = lat_tables(256, 384)
    perm_f, perm_b = permutation(32, 4)
    cot = cotangent[0]
    any_spec = pl.BlockSpec(memory_space=pl.ANY)
    vmem = pl.BlockSpec(memory_space=pltpu.VMEM)
    wide = (1024, 768)
    rows, grads = pl.pallas_call(
        functools.partial(main_kernel, factor, norm),
        out_shape=(
            jax.ShapeDtypeStruct((3072, 384), BF),
            jax.ShapeDtypeStruct((32, 5, 8, 128), F32),
        ),
        in_specs=[any_spec] * 6 + [vmem] * 5,
        out_specs=(any_spec, vmem),
        scratch_shapes=[
            pltpu.VMEM((6, 768, 384), BF), pltpu.VMEM((6, 768, 384), BF),
            pltpu.VMEM((256, 4, 384), jnp.int32),
            pltpu.VMEM((512, 768), BF), pltpu.VMEM((512, 768), BF), pltpu.VMEM((768, 512), BF),
            pltpu.VMEM((3, 64, 16, 384), BF), pltpu.VMEM((3, 64, 16, 384), BF), pltpu.VMEM((3072, 384), BF),
            pltpu.VMEM((3072, 384), BF), pltpu.VMEM((3072, 384), BF),
            pltpu.VMEM((4, 768, 384), BF),
            pltpu.VMEM(wide, BF), pltpu.VMEM(wide, BF), pltpu.VMEM(wide, BF), pltpu.VMEM(wide, BF),
            pltpu.VMEM((4, 512, 384), BF),
            pltpu.VMEM(wide, BF), pltpu.VMEM(wide, BF),
            pltpu.VMEM((768, 768), BF), pltpu.VMEM((768, 768), BF), pltpu.VMEM((768, 768), BF),
            pltpu.VMEM((384, 768), F32), pltpu.VMEM((384, 768), F32), pltpu.VMEM((8, 768), F32),
            pltpu.VMEM((96, 768), F32),
            pltpu.VMEM((32, 5, 8, 128), F32), pltpu.VMEM((32, 5, 8, 128), F32), pltpu.VMEM((32, 5, 8, 128), F32),
            pltpu.VMEM((8, 5, 8, 128), F32), pltpu.VMEM((5, 8, 128), F32), pltpu.VMEM((5, 8, 128), F32),
            pltpu.SemaphoreType.DMA((8,)), pltpu.SemaphoreType.DMA((6,)), pltpu.SemaphoreType.DMA((6,)),
        ],
        compiler_params=pltpu.CompilerParams(
            collective_id=0, has_side_effects=True, vmem_limit_bytes=58 * MIB
        ),
        name="exchange",
    )(cot, inputs[0], masks[0], lon, lat_f, lat_b, perm_f, perm_b, w_first, b_first, w_second)
    whole = lambda shape: pl.BlockSpec(shape, lambda i: (0,) * len(shape))
    field, w1, b1, w2, b2 = pl.pallas_call(
        functools.partial(last_kernel, factor),
        out_shape=(
            jax.ShapeDtypeStruct((6, 768, 384), BF),
            jax.ShapeDtypeStruct((2, 4, 96, 96), F32),
            jax.ShapeDtypeStruct((2, 384), F32),
            jax.ShapeDtypeStruct((2, 4, 96, 96), F32),
            jax.ShapeDtypeStruct((2, 384), F32),
        ),
        grid=(3,),
        in_specs=[
            pl.BlockSpec((64, 1, 16, 384), lambda i: (0, i, 0, 0)),
            pl.BlockSpec((2, 768, 384), lambda i: (i, 0, 0)),
            whole((768, 512)),
            whole((32, 5, 8, 128)),
        ],
        out_specs=(
            pl.BlockSpec((2, 768, 384), lambda i: (i, 0, 0)),
            whole((2, 4, 96, 96)), whole((2, 384)), whole((2, 4, 96, 96)), whole((2, 384)),
        ),
        compiler_params=pltpu.CompilerParams(vmem_limit_bytes=48 * MIB),
        name="field",
    )(rows.reshape(64, 3, 16, 384), cot, lon_t, grads)
    return field[None], w1, b1, w2, b2


def solution(mesh):
    placed = (
        P("dp", "sp", None, None),
        P("dp", "sp", None, None),
        P("dp", None, "sp", None),
        P(),
        P(),
        P(),
    )
    return jax.shard_map(
        local,
        mesh=mesh,
        in_specs=placed,
        out_specs=(P("dp", "sp", None, None), P(), P(), P(), P()),
        check_vma=False,
    )
```

```python
import functools
import math

import jax
import jax.numpy as jnp
import ml_dtypes
import numpy as np
from jax import lax
from jax.experimental import pallas as pl
from jax.experimental.pallas import tpu as pltpu
from jax.sharding import PartitionSpec as P

MESH = pl.DeviceIdType.MESH
BF = jnp.bfloat16
F32 = jnp.float32
MIB = 2**20
AHEAD = 24


def bf(array):
    return array.astype(np.float32).astype(ml_dtypes.bfloat16)


def lon_tables(count, length, devices):
    phase = (np.arange(count)[:, None] * np.arange(length)[None, :]) % length
    angle = (np.float32(2.0 * math.pi / length) * phase.astype(np.float32)).astype(np.float64)
    table = np.stack([np.cos(angle), -np.sin(angle)], 1).reshape(2 * count, length)
    return bf(table), bf(table.T)


def lat_tables(keep, length):
    index = np.arange(keep)
    modes = np.where(index < keep // 2, index, index + (length - keep))
    phase = (modes[:, None] * np.arange(length)[None, :]) % length
    angle = (np.float32(2.0 * math.pi / length) * phase.astype(np.float32)).astype(np.float64)
    cosine, sine = np.cos(angle), np.sin(angle)
    forward = np.stack([np.stack([cosine, sine], 2), np.stack([-sine, cosine], 2)])
    forward = forward.reshape(2 * keep, 2 * length)
    backward = forward.T.reshape(4, 2, 8, 12, 2 * keep).transpose(1, 0, 2, 3, 4)
    return bf(forward), bf(backward.reshape(2 * length, 2 * keep))


def permutation(rows, modes):
    out = np.zeros((modes, rows, 2, rows, modes, 2), np.float32)
    for k in range(modes):
        for h in range(rows):
            for p in range(2):
                out[k, h, p, h, k, p] = 1.0
    size = modes * rows * 2
    out = out.reshape(size, size)
    return bf(out), bf(out.T)


def dot(left, right):
    return jnp.dot(left, right, preferred_element_type=F32)


def dot_tn(left, right):
    return lax.dot_general(left, right, (((0,), (0,)), ((), ())), preferred_element_type=F32)


def main_kernel(
    factor, norm,
    cot_hbm, inp_hbm, mask_hbm, lon_hbm, latf_hbm, latb_hbm, pf_hbm, pb_hbm, w1_hbm, b1_hbm, w2_hbm,
    rows_out, grads_out,
    cot_v, inp_v, mask_v, lon_v, latf_v, latb_v, pf_ref, pb_ref, w1_ref, b1_ref, w2_ref,
    send_c, send_i, send_r, relay, recv_c, recv_i, xt, spec, dtwo, done, hid, dsp, relu, shrink,
    m1, m2, m3, acc_a, acc_b, acc_s, fold, parts, gathered, plane, column, chunk, result,
    lsem, ssem, rsem,
):
    dp = lax.axis_index("dp")
    me = lax.axis_index("sp")
    x = me // 16
    z_hi = (me // 8) % 2
    low = me % 8
    p1 = x * 8 + low
    zi = z_hi * 4 + dp

    loads = [
        pltpu.make_async_copy(there, here, lsem.at[i])
        for i, (there, here) in enumerate((
            (lon_hbm.at[pl.ds(0, 256)], lon_v.at[pl.ds(0, 256)]),
            (cot_hbm.at[0], cot_v.at[0]),
            (cot_hbm.at[1], cot_v.at[1]),
            (lon_hbm.at[pl.ds(256, 256)], lon_v.at[pl.ds(256, 256)]),
            (cot_hbm.at[pl.ds(2, 4)], cot_v.at[pl.ds(2, 4)]),
            (inp_hbm, inp_v),
            (w1_hbm, w1_ref), (w2_hbm, w2_ref), (b1_hbm, b1_ref),
            (mask_hbm, mask_v), (latf_hbm, latf_v), (latb_hbm, latb_v), (pf_hbm, pf_ref), (pb_hbm, pb_ref),
        ))
    ]
    for load in loads:
        load.start()

    barrier = pltpu.get_barrier_semaphore()

    def greet(o, carry):
        pl.semaphore_signal(barrier, inc=1, device_id=(dp, (me + o) % 64), device_id_type=MESH)
        return carry

    lax.fori_loop(1, 64, greet, 0)
    for o in range(1, 4):
        for zh in range(2):
            pl.semaphore_signal(
                barrier, inc=1, device_id=((dp + o) % 4, x * 16 + zh * 8 + low), device_id_type=MESH
            )

    def transform(field, send, hp):
        def part(m, carry):
            table = lon_v[pl.ds(pl.multiple_of(m * 128, 128), 128), :]
            first = dot(table, field[2 * hp]).reshape(16, 8, 384)
            second = dot(table, field[2 * hp + 1]).reshape(16, 8, 384)
            send[hp, pl.ds(m * 16, 16)] = jnp.concatenate([first, second], axis=1).astype(BF)
            return carry

        lax.fori_loop(0, 4, part, 0)

    def send_rows(send, recv, slot, hp):
        place = pl.ds(pl.multiple_of(me * 48 + hp * 16, 16), 16)
        recv[place, :] = send[hp, me]

        def one(o, carry):
            there = (me + o) % 64
            pltpu.make_async_remote_copy(
                src_ref=send.at[hp, there], dst_ref=recv.at[place], send_sem=ssem.at[slot],
                recv_sem=rsem.at[slot], device_id=(dp, there), device_id_type=MESH,
            ).start()
            return carry

        lax.fori_loop(1, 64, one, 0)

    for load in loads[:4]:
        load.wait()
    transform(cot_v, send_c, 0)
    pl.semaphore_wait(barrier, 69)
    send_rows(send_c, recv_c, 0, 0)
    loads[4].wait()

    def cot_pair(hp, carry):
        transform(cot_v, send_c, hp)
        send_rows(send_c, recv_c, 0, hp)
        return carry

    lax.fori_loop(1, 3, cot_pair, 0)
    loads[5].wait()

    def inp_pair(hp, carry):
        transform(inp_v, send_i, hp)
        send_rows(send_i, recv_i, 1, hp)
        return carry

    lax.fori_loop(0, 3, inp_pair, 0)

    for load in loads[6:]:
        load.wait()

    lane = lax.broadcasted_iota(jnp.int32, (96, 384), 1)
    row = lax.broadcasted_iota(jnp.int32, (96, 384), 0)
    for b in range(4):
        place = (lane == row + 96 * b).astype(BF)
        up = slice(96 * b, 96 * b + 96)
        dn = slice(384 + 96 * b, 384 + 96 * b + 96)
        w1r, w1i = w1_ref[0, b], w1_ref[1, b]
        w2r, w2i = w2_ref[0, b], w2_ref[1, b]
        real, imag = dot(w1r, place).astype(BF), dot(w1i, place).astype(BF)
        m1[up, 0:384] = real
        m1[up, 384:768] = imag
        m1[dn, 0:384] = -imag
        m1[dn, 384:768] = real
        for target, wr, wi in ((m2, w2r, w2i), (m3, w1r, w1i)):
            real, imag = dot_tn(wr, place).astype(BF), dot_tn(wi, place).astype(BF)
            target[up, 0:384] = real
            target[up, 384:768] = -imag
            target[dn, 0:384] = imag
            target[dn, 384:768] = real
    for kk in range(4):
        bits = mask_v[:, kk, :]
        here = slice(256 * kk, 256 * kk + 256)
        relu[here, 0:384] = (bits & 1).astype(F32).astype(BF)
        relu[here, 384:768] = ((bits >> 1) & 1).astype(F32).astype(BF)
        shrink[here, 0:384] = ((bits >> 2) & 1).astype(F32).astype(BF)
        shrink[here, 384:768] = ((bits >> 3) & 1).astype(F32).astype(BF)

    def arrived(recv, slot):
        view = recv.at[pl.ds(0, 63 * 48)]
        pltpu.make_async_remote_copy(
            src_ref=view, dst_ref=view, send_sem=ssem.at[slot], recv_sem=rsem.at[slot],
            device_id=(dp, me), device_id_type=MESH,
        ).wait_recv()

    def by_mode(recv):
        def block(g, carry):
            rows = dot(pf_ref[...], recv[pl.ds(pl.multiple_of(g * 256, 256), 256), :]).astype(BF)
            for kk in range(4):
                xt[kk, pl.ds(pl.multiple_of(g * 64, 64), 64), :] = rows[64 * kk:64 * kk + 64]
            return carry

        lax.fori_loop(0, 12, block, 0)

    def mode_rows(kk):
        return pl.ds(pl.multiple_of(kk * 256, 256), 256)

    arrived(recv_c, 0)
    by_mode(recv_c)

    def adjoint(kk, carry):
        here = mode_rows(kk)
        scale = jnp.where(me * 4 + kk == 0, factor, 2.0 * factor).astype(F32)
        for q in range(2):
            cols = slice(384 * q, 384 * q + 384)
            d_out = (dot(latf_v[256 * q:256 * q + 256, :], xt[kk]) * scale).astype(BF)
            dtwo[here, cols] = d_out * shrink[here, cols]
        back = dot(dtwo[here, :], m2[...]) * relu[here, :].astype(F32)
        done[here, :] = back.astype(BF)
        d_spec = dot(done[here, :], m3[...]).astype(BF)
        dsp[kk, 0:256, :] = d_spec[:, 0:384]
        dsp[kk, 256:512, :] = d_spec[:, 384:768]
        return carry

    lax.fori_loop(0, 4, adjoint, 0)

    def image_quarter(m):
        def block(b, carry):
            table = latb_v[pl.ds(pl.multiple_of(m * 192 + b * 64, 64), 64), :]
            image = jnp.concatenate([dot(table, dsp[kk]).astype(BF) for kk in range(4)], axis=0)
            place = pl.ds(pl.multiple_of(m * 768 + b * 256, 256), 256)
            send_r[place, :] = dot(pb_ref[...], image).astype(BF)
            return carry

        lax.fori_loop(0, 3, block, 0)

    def rows48(index):
        return pl.ds(pl.multiple_of(index * 48, 16), 48)

    def in_plane(p):
        return (p // 8) * 16 + z_hi * 8 + p % 8

    other = me + 8 - 16 * z_hi
    mine = z_hi * 32
    theirs = 32 - mine

    def send_in_plane(base, target, slot):
        def one(o, carry):
            p = (p1 + o) % 32
            pltpu.make_async_remote_copy(
                src_ref=send_r.at[rows48(base + p)], dst_ref=target, send_sem=ssem.at[6],
                recv_sem=rsem.at[slot], device_id=(dp, in_plane(p)), device_id_type=MESH,
            ).start()
            return carry

        lax.fori_loop(1, 32, one, 0)

    def send_across(first, last):
        def one(p, carry):
            pltpu.make_async_remote_copy(
                src_ref=relay.at[rows48(p)], dst_ref=rows_out.at[rows48(in_plane(p))],
                send_sem=ssem.at[7], recv_sem=rsem.at[2],
                device_id=(dp, other), device_id_type=MESH,
            ).start()
            return carry

        lax.fori_loop(first, last, one, 0)

    image_quarter(theirs // 16)
    image_quarter(theirs // 16 + 1)
    send_in_plane(theirs, relay.at[rows48(p1)], 6)
    relay[rows48(p1), :] = send_r[rows48(theirs + p1), :]
    image_quarter(mine // 16)
    image_quarter(mine // 16 + 1)
    own = pltpu.make_async_copy(send_r.at[rows48(mine + p1)], rows_out.at[rows48(me)], lsem.at[14])
    own.start()
    send_in_plane(mine, rows_out.at[rows48(me)], 2)

    arrived(recv_i, 1)
    view = relay.at[pl.ds(0, 31 * 48)]
    pltpu.make_async_remote_copy(
        src_ref=view, dst_ref=view, send_sem=ssem.at[6], recv_sem=rsem.at[6],
        device_id=(dp, me), device_id_type=MESH,
    ).wait_recv()
    send_across(0, AHEAD)
    by_mode(recv_i)

    def layer(kk, carry):
        here = mode_rows(kk)
        for q in range(2):
            cols = slice(384 * q, 384 * q + 384)
            spec[here, cols] = (dot(latf_v[256 * q:256 * q + 256, :], xt[kk]) * factor).astype(BF)
        pre = dot(spec[here, :], m1[...])
        for q in range(2):
            cols = slice(384 * q, 384 * q + 384)
            kept = (pre[:, cols] + b1_ref[q:q + 1, :]) * relu[here, cols].astype(F32)
            hid[here, cols] = kept.astype(BF)
        return carry

    lax.fori_loop(0, 4, layer, 0)

    lanes = lax.broadcasted_iota(jnp.int32, (96, 384), 1) // 96
    for which, (left, right) in enumerate(((spec, done), (hid, dtwo))):
        acc_a[...] = jnp.zeros_like(acc_a)
        acc_b[...] = jnp.zeros_like(acc_b)
        acc_s[...] = jnp.zeros_like(acc_s)

        def add(kk, carry, left=left, right=right):
            here = mode_rows(kk)
            r = right[here, :]
            acc_a[...] += dot_tn(left[here, 0:384], r)
            acc_b[...] += dot_tn(left[here, 384:768], r)
            acc_s[...] += dot(jnp.ones((8, 256), BF), r)
            return carry

        lax.fori_loop(0, 4, add, 0)
        real = jnp.zeros((96, 384), F32)
        imag = jnp.zeros((96, 384), F32)
        for b in range(4):
            up = slice(96 * b, 96 * b + 96)
            real = jnp.where(lanes == b, acc_a[up, 0:384] + acc_b[up, 384:768], real)
            imag = jnp.where(lanes == b, acc_a[up, 384:768] - acc_b[up, 0:384], imag)
        fold[0:96, 0:384] = real
        fold[0:96, 384:768] = imag
        for r in range(12):
            for c in range(6):
                t = which * 72 + r * 6 + c
                parts[t // 5, t % 5] = fold[8 * r:8 * r + 8, 128 * c:128 * c + 128]
        for c in range(6):
            t = 144 + c
            sums = acc_s[:, 128 * c:128 * c + 128]
            if which == 0:
                parts[t // 5, t % 5] = sums
            else:
                first = lax.broadcasted_iota(jnp.int32, (8, 128), 0) == 0
                parts[t // 5, t % 5] = jnp.where(first, parts[t // 5, t % 5], sums)
    for t in range(150, 160):
        parts[t // 5, t % 5] = jnp.zeros((8, 128), F32)

    def wait_all(ref, count, slot):
        view = ref.at[pl.ds(0, count)]
        pltpu.make_async_remote_copy(
            src_ref=view, dst_ref=view, send_sem=ssem.at[slot], recv_sem=rsem.at[slot],
            device_id=(dp, me), device_id_type=MESH,
        ).wait()

    plane[p1] = parts[p1]

    def scatter(o, carry):
        p = (p1 + o) % 32
        pltpu.make_async_remote_copy(
            src_ref=parts.at[p], dst_ref=plane.at[p1], send_sem=ssem.at[3], recv_sem=rsem.at[3],
            device_id=(dp, in_plane(p)), device_id_type=MESH,
        ).start()
        return carry

    lax.fori_loop(1, 32, scatter, 0)
    wait_all(plane, 31, 3)
    chunk[...] = plane[0]

    def add_plane(p, carry):
        chunk[...] += plane[p]
        return carry

    lax.fori_loop(1, 32, add_plane, 0)
    column[zi] = chunk[...]

    def along_z(o, carry):
        z = (zi + o) % 8
        pltpu.make_async_remote_copy(
            src_ref=chunk, dst_ref=column.at[zi], send_sem=ssem.at[4], recv_sem=rsem.at[4],
            device_id=(z % 4, x * 16 + (z // 4) * 8 + low), device_id_type=MESH,
        ).start()
        return carry

    lax.fori_loop(1, 8, along_z, 0)
    send_across(AHEAD, 32)
    wait_all(column, 7, 4)
    total = column[0]
    for z in range(1, 8):
        total = total + column[z]
    result[...] = total * norm
    gathered[p1] = result[...]

    def gather(o, carry):
        p = (p1 + o) % 32
        pltpu.make_async_remote_copy(
            src_ref=result, dst_ref=gathered.at[p1], send_sem=ssem.at[5], recv_sem=rsem.at[5],
            device_id=(dp, in_plane(p)), device_id_type=MESH,
        ).start()
        return carry

    lax.fori_loop(1, 32, gather, 0)
    wait_all(gathered, 31, 5)
    grads = pltpu.make_async_copy(gathered, grads_out, lsem.at[15])
    grads.start()

    grads.wait()
    own.wait()
    arrived(rows_out, 2)
    for slot, count in ((0, 63), (1, 63), (6, 62), (7, 32)):
        view = recv_c.at[pl.ds(0, count * 48)]
        pltpu.make_async_remote_copy(
            src_ref=view, dst_ref=view, send_sem=ssem.at[slot], recv_sem=rsem.at[slot],
            device_id=(dp, me), device_id_type=MESH,
        ).wait_send()


def last_kernel(
    factor, rows_hbm, cot_hbm, table_hbm, grads_hbm, out_hbm, w1_hbm, b1_hbm, w2_hbm, b2_hbm,
    rows_v, cot_v, table_v, grads_v, out_v, w1_v, b1_v, w2_v, b2_v, rsem, csem, tsem, osem, gsem,
):
    table_load = [
        pltpu.make_async_copy(table_hbm.at[pl.ds(256 * m, 256)], table_v.at[pl.ds(256 * m, 256)], tsem.at[m])
        for m in range(3)
    ]
    rows_load = [
        [
            pltpu.make_async_copy(
                rows_hbm.at[pl.ds(32 * s, 32), hp], rows_v.at[hp, pl.ds(32 * s, 32)], rsem.at[hp, s]
            )
            for s in range(2)
        ]
        for hp in range(3)
    ]
    cot_load = [pltpu.make_async_copy(cot_hbm.at[h], cot_v.at[h], csem.at[h]) for h in range(6)]
    grads_load = pltpu.make_async_copy(grads_hbm, grads_v, gsem.at[0])
    for load in rows_load[0]:
        load.start()
    for load in table_load:
        load.start()
    for hp in range(3):
        cot_load[2 * hp].start()
        cot_load[2 * hp + 1].start()
        if hp == 0:
            grads_load.start()
        if hp < 2:
            for load in rows_load[hp + 1]:
                load.start()

    stores = [pltpu.make_async_copy(out_v.at[h], out_hbm.at[h], osem.at[h]) for h in range(6)]
    small = [
        pltpu.make_async_copy(here, there, gsem.at[1 + i])
        for i, (here, there) in enumerate(((w1_v, w1_hbm), (b1_v, b1_hbm), (w2_v, w2_hbm), (b2_v, b2_hbm)))
    ]

    def tiles(first):
        return jnp.concatenate([grads_v[t // 5, t % 5] for t in range(first, first + 6)], axis=1)

    for hp in range(3):
        for load in rows_load[hp]:
            load.wait()
        rows = rows_v[hp].astype(F32)
        for half in range(2):
            image = rows[:, 8 * half:8 * half + 8, :].reshape(512, 384).astype(BF)
            if half == 0:
                first = image
        for h in (2 * hp, 2 * hp + 1):
            cot_load[h].wait()
        pair = jnp.concatenate([first, image], axis=1)
        for m in range(3):
            if hp == 0:
                table_load[m].wait()
            part = slice(256 * m, 256 * m + 256)
            field = dot(table_v[part, :], pair) * factor
            for half in range(2):
                h = 2 * hp + half
                cols = slice(384 * half, 384 * half + 384)
                out_v[h, part, :] = (cot_v[h, part, :].astype(F32) + field[:, cols]).astype(BF)
        for h in (2 * hp, 2 * hp + 1):
            stores[h].start()
        if hp == 0:
            grads_load.wait()
            for which, out in enumerate((w1_v, w2_v)):
                for r in range(12):
                    line = tiles(which * 72 + r * 6)
                    for q in range(2):
                        for b in range(4):
                            start = q * 384 + b * 96
                            out[q, b, 8 * r:8 * r + 8, :] = line[:, start:start + 96]
            line = tiles(144)
            for which, out in enumerate((b1_v, b2_v)):
                for q in range(2):
                    out[q:q + 1, :] = line[which:which + 1, 384 * q:384 * q + 384]
            for copy in small:
                copy.start()
    for copy in small + stores:
        copy.wait()


def last_call(factor, rows, cot, table, grads):
    any_spec = pl.BlockSpec(memory_space=pl.ANY)
    small = [(2, 4, 96, 96), (2, 384)] * 2
    return pl.pallas_call(
        functools.partial(last_kernel, factor),
        out_shape=(jax.ShapeDtypeStruct((6, 768, 384), BF),) + tuple(jax.ShapeDtypeStruct(s, F32) for s in small),
        in_specs=[any_spec] * 4,
        out_specs=(any_spec,) * 5,
        scratch_shapes=[
            pltpu.VMEM((3, 64, 16, 384), BF), pltpu.VMEM((6, 768, 384), BF), pltpu.VMEM((768, 512), BF),
            pltpu.VMEM((32, 5, 8, 128), F32), pltpu.VMEM((6, 768, 384), BF),
        ] + [pltpu.VMEM(s, F32) for s in small] + [
            pltpu.SemaphoreType.DMA((3, 2)), pltpu.SemaphoreType.DMA((6,)), pltpu.SemaphoreType.DMA((3,)),
            pltpu.SemaphoreType.DMA((6,)), pltpu.SemaphoreType.DMA((5,)),
        ],
        compiler_params=pltpu.CompilerParams(vmem_limit_bytes=62 * MIB),
        name="field",
    )(rows, cot, table, grads)


def local(inputs, cotangent, masks, w_first, b_first, w_second):
    factor = 1.0 / math.sqrt(384 * 768)
    norm = 1.0 / math.sqrt(4 * 256 * 256)
    lon, lon_t = lon_tables(256, 768, 64)
    lat_f, lat_b = lat_tables(256, 384)
    perm_f, perm_b = permutation(32, 4)
    cot = cotangent[0]
    any_spec = pl.BlockSpec(memory_space=pl.ANY)
    wide = (1024, 768)
    rows, grads = pl.pallas_call(
        functools.partial(main_kernel, factor, norm),
        out_shape=(
            jax.ShapeDtypeStruct((3072, 384), BF),
            jax.ShapeDtypeStruct((32, 5, 8, 128), F32),
        ),
        in_specs=[any_spec] * 11,
        out_specs=(any_spec, any_spec),
        scratch_shapes=[
            pltpu.VMEM((6, 768, 384), BF), pltpu.VMEM((6, 768, 384), BF),
            pltpu.VMEM((256, 4, 384), jnp.int32),
            pltpu.VMEM((512, 768), BF), pltpu.VMEM((512, 768), BF), pltpu.VMEM((768, 512), BF),
            pltpu.VMEM((256, 256), BF), pltpu.VMEM((256, 256), BF),
            pltpu.VMEM((2, 4, 96, 96), BF), pltpu.VMEM((2, 384), F32), pltpu.VMEM((2, 4, 96, 96), BF),
            pltpu.VMEM((3, 64, 16, 384), BF), pltpu.VMEM((3, 64, 16, 384), BF), pltpu.VMEM((3072, 384), BF), pltpu.VMEM((1536, 384), BF),
            pltpu.VMEM((3072, 384), BF), pltpu.VMEM((3072, 384), BF),
            pltpu.VMEM((4, 768, 384), BF),
            pltpu.VMEM(wide, BF), pltpu.VMEM(wide, BF), pltpu.VMEM(wide, BF), pltpu.VMEM(wide, BF),
            pltpu.VMEM((4, 512, 384), BF),
            pltpu.VMEM(wide, BF), pltpu.VMEM(wide, BF),
            pltpu.VMEM((768, 768), BF), pltpu.VMEM((768, 768), BF), pltpu.VMEM((768, 768), BF),
            pltpu.VMEM((384, 768), F32), pltpu.VMEM((384, 768), F32), pltpu.VMEM((8, 768), F32),
            pltpu.VMEM((96, 768), F32),
            pltpu.VMEM((32, 5, 8, 128), F32), pltpu.VMEM((32, 5, 8, 128), F32), pltpu.VMEM((32, 5, 8, 128), F32),
            pltpu.VMEM((8, 5, 8, 128), F32), pltpu.VMEM((5, 8, 128), F32), pltpu.VMEM((5, 8, 128), F32),
            pltpu.SemaphoreType.DMA((16,)), pltpu.SemaphoreType.DMA((8,)), pltpu.SemaphoreType.DMA((7,)),
        ],
        compiler_params=pltpu.CompilerParams(
            collective_id=0, has_side_effects=True, vmem_limit_bytes=62 * MIB
        ),
        name="exchange",
    )(cot, inputs[0], masks[0], lon, lat_f, lat_b, perm_f, perm_b, w_first, b_first, w_second)
    field, w1, b1, w2, b2 = last_call(factor, rows.reshape(64, 3, 16, 384), cot, lon_t, grads)
    return field[None], w1, b1, w2, b2


def solution(mesh):
    placed = (
        P("dp", "sp", None, None),
        P("dp", "sp", None, None),
        P("dp", None, "sp", None),
        P(),
        P(),
        P(),
    )
    return jax.shard_map(
        local,
        mesh=mesh,
        in_specs=placed,
        out_specs=(P("dp", "sp", None, None), P(), P(), P(), P()),
        check_vma=False,
    )
```

```python
import functools
import math

import jax
import jax.numpy as jnp
import ml_dtypes
import numpy as np
from jax import lax
from jax.experimental import pallas as pl
from jax.experimental.pallas import tpu as pltpu
from jax.sharding import PartitionSpec as P

MESH = pl.DeviceIdType.MESH
BF = jnp.bfloat16
F32 = jnp.float32
MIB = 2**20
AHEAD = 20
DIRECT = 8


def bf(array):
    return array.astype(np.float32).astype(ml_dtypes.bfloat16)


def lon_tables(count, length, devices):
    phase = (np.arange(count)[:, None] * np.arange(length)[None, :]) % length
    angle = (np.float32(2.0 * math.pi / length) * phase.astype(np.float32)).astype(np.float64)
    table = np.stack([np.cos(angle), -np.sin(angle)], 1).reshape(2 * count, length)
    return bf(table), bf(table.T)


def lat_tables(keep, length):
    index = np.arange(keep)
    modes = np.where(index < keep // 2, index, index + (length - keep))
    phase = (modes[:, None] * np.arange(length)[None, :]) % length
    angle = (np.float32(2.0 * math.pi / length) * phase.astype(np.float32)).astype(np.float64)
    cosine, sine = np.cos(angle), np.sin(angle)
    forward = np.stack([np.stack([cosine, sine], 2), np.stack([-sine, cosine], 2)])
    forward = forward.reshape(2 * keep, 2 * length)
    backward = forward.T.reshape(4, 2, 8, 12, 2 * keep).transpose(1, 0, 2, 3, 4)
    return bf(forward), bf(backward.reshape(2 * length, 2 * keep))


def permutation(rows, modes):
    out = np.zeros((modes, rows, 2, rows, modes, 2), np.float32)
    for k in range(modes):
        for h in range(rows):
            for p in range(2):
                out[k, h, p, h, k, p] = 1.0
    size = modes * rows * 2
    out = out.reshape(size, size)
    return bf(out), bf(out.T)


def dot(left, right):
    return jnp.dot(left, right, preferred_element_type=F32)


def dot_tn(left, right):
    return lax.dot_general(left, right, (((0,), (0,)), ((), ())), preferred_element_type=F32)


def main_kernel(
    factor, norm,
    cot_hbm, inp_hbm, mask_hbm, lon_hbm, latf_hbm, latb_hbm, pf_hbm, pb_hbm, w1_hbm, b1_hbm, w2_hbm,
    rows_out, grads_out,
    cot_v, inp_v, mask_v, lon_v, latf_v, latb_v, pf_ref, pb_ref, w1_ref, b1_ref, w2_ref,
    send_c, send_i, send_r, relay, recv_c, recv_i, xt, spec, dtwo, done, hid, dsp, relu, shrink,
    m1, m2, m3, acc_a, acc_b, acc_s, fold, parts, gathered, plane, column, chunk, result,
    lsem, ssem, rsem,
):
    dp = lax.axis_index("dp")
    me = lax.axis_index("sp")
    x = me // 16
    z_hi = (me // 8) % 2
    low = me % 8
    p1 = x * 8 + low
    zi = z_hi * 4 + dp

    loads = [
        pltpu.make_async_copy(there, here, lsem.at[i])
        for i, (there, here) in enumerate((
            (lon_hbm.at[pl.ds(0, 256)], lon_v.at[pl.ds(0, 256)]),
            (cot_hbm.at[0], cot_v.at[0]),
            (cot_hbm.at[1], cot_v.at[1]),
            (lon_hbm.at[pl.ds(256, 256)], lon_v.at[pl.ds(256, 256)]),
            (cot_hbm.at[pl.ds(2, 4)], cot_v.at[pl.ds(2, 4)]),
            (inp_hbm, inp_v),
            (w1_hbm, w1_ref), (w2_hbm, w2_ref), (b1_hbm, b1_ref),
            (mask_hbm, mask_v), (latf_hbm, latf_v), (latb_hbm, latb_v), (pf_hbm, pf_ref), (pb_hbm, pb_ref),
        ))
    ]
    for load in loads:
        load.start()

    barrier = pltpu.get_barrier_semaphore()

    def greet(o, carry):
        pl.semaphore_signal(barrier, inc=1, device_id=(dp, (me + o) % 64), device_id_type=MESH)
        return carry

    lax.fori_loop(1, 64, greet, 0)
    for o in range(1, 4):
        for zh in range(2):
            pl.semaphore_signal(
                barrier, inc=1, device_id=((dp + o) % 4, x * 16 + zh * 8 + low), device_id_type=MESH
            )

    def transform(field, send, hp):
        def part(m, carry):
            table = lon_v[pl.ds(pl.multiple_of(m * 128, 128), 128), :]
            first = dot(table, field[2 * hp]).reshape(16, 8, 384)
            second = dot(table, field[2 * hp + 1]).reshape(16, 8, 384)
            send[hp, pl.ds(m * 16, 16)] = jnp.concatenate([first, second], axis=1).astype(BF)
            return carry

        lax.fori_loop(0, 4, part, 0)

    def send_rows(send, recv, slot, hp):
        place = pl.ds(pl.multiple_of(me * 48 + hp * 16, 16), 16)
        recv[place, :] = send[hp, me]

        def one(o, carry):
            there = (me + o) % 64
            pltpu.make_async_remote_copy(
                src_ref=send.at[hp, there], dst_ref=recv.at[place], send_sem=ssem.at[slot],
                recv_sem=rsem.at[slot], device_id=(dp, there), device_id_type=MESH,
            ).start()
            return carry

        lax.fori_loop(1, 64, one, 0)

    for load in loads[:4]:
        load.wait()
    transform(cot_v, send_c, 0)
    pl.semaphore_wait(barrier, 69)
    send_rows(send_c, recv_c, 0, 0)
    loads[4].wait()

    def cot_pair(hp, carry):
        transform(cot_v, send_c, hp)
        send_rows(send_c, recv_c, 0, hp)
        return carry

    lax.fori_loop(1, 3, cot_pair, 0)
    loads[5].wait()

    def inp_pair(hp, carry):
        transform(inp_v, send_i, hp)
        send_rows(send_i, recv_i, 1, hp)
        return carry

    lax.fori_loop(0, 3, inp_pair, 0)

    for load in loads[6:]:
        load.wait()

    lane = lax.broadcasted_iota(jnp.int32, (96, 384), 1)
    row = lax.broadcasted_iota(jnp.int32, (96, 384), 0)
    for b in range(4):
        place = (lane == row + 96 * b).astype(BF)
        up = slice(96 * b, 96 * b + 96)
        dn = slice(384 + 96 * b, 384 + 96 * b + 96)
        w1r, w1i = w1_ref[0, b], w1_ref[1, b]
        w2r, w2i = w2_ref[0, b], w2_ref[1, b]
        real, imag = dot(w1r, place).astype(BF), dot(w1i, place).astype(BF)
        m1[up, 0:384] = real
        m1[up, 384:768] = imag
        m1[dn, 0:384] = -imag
        m1[dn, 384:768] = real
        for target, wr, wi in ((m2, w2r, w2i), (m3, w1r, w1i)):
            real, imag = dot_tn(wr, place).astype(BF), dot_tn(wi, place).astype(BF)
            target[up, 0:384] = real
            target[up, 384:768] = -imag
            target[dn, 0:384] = imag
            target[dn, 384:768] = real
    for kk in range(4):
        bits = mask_v[:, kk, :]
        here = slice(256 * kk, 256 * kk + 256)
        relu[here, 0:384] = (bits & 1).astype(F32).astype(BF)
        relu[here, 384:768] = ((bits >> 1) & 1).astype(F32).astype(BF)
        shrink[here, 0:384] = ((bits >> 2) & 1).astype(F32).astype(BF)
        shrink[here, 384:768] = ((bits >> 3) & 1).astype(F32).astype(BF)

    def arrived(recv, slot):
        view = recv.at[pl.ds(0, 63 * 48)]
        pltpu.make_async_remote_copy(
            src_ref=view, dst_ref=view, send_sem=ssem.at[slot], recv_sem=rsem.at[slot],
            device_id=(dp, me), device_id_type=MESH,
        ).wait_recv()

    def by_mode(recv):
        def block(g, carry):
            rows = dot(pf_ref[...], recv[pl.ds(pl.multiple_of(g * 256, 256), 256), :]).astype(BF)
            for kk in range(4):
                xt[kk, pl.ds(pl.multiple_of(g * 64, 64), 64), :] = rows[64 * kk:64 * kk + 64]
            return carry

        lax.fori_loop(0, 12, block, 0)

    def mode_rows(kk):
        return pl.ds(pl.multiple_of(kk * 256, 256), 256)

    arrived(recv_c, 0)
    by_mode(recv_c)

    def adjoint(kk, carry):
        here = mode_rows(kk)
        scale = jnp.where(me * 4 + kk == 0, factor, 2.0 * factor).astype(F32)
        for q in range(2):
            cols = slice(384 * q, 384 * q + 384)
            d_out = (dot(latf_v[256 * q:256 * q + 256, :], xt[kk]) * scale).astype(BF)
            dtwo[here, cols] = d_out * shrink[here, cols]
        back = dot(dtwo[here, :], m2[...]) * relu[here, :].astype(F32)
        done[here, :] = back.astype(BF)
        d_spec = dot(done[here, :], m3[...]).astype(BF)
        dsp[kk, 0:256, :] = d_spec[:, 0:384]
        dsp[kk, 256:512, :] = d_spec[:, 384:768]
        return carry

    lax.fori_loop(0, 4, adjoint, 0)

    def image_quarter(m):
        def block(b, carry):
            table = latb_v[pl.ds(pl.multiple_of(m * 192 + b * 64, 64), 64), :]
            image = jnp.concatenate([dot(table, dsp[kk]).astype(BF) for kk in range(4)], axis=0)
            place = pl.ds(pl.multiple_of(m * 768 + b * 256, 256), 256)
            send_r[place, :] = dot(pb_ref[...], image).astype(BF)
            return carry

        lax.fori_loop(0, 3, block, 0)

    def rows48(index):
        return pl.ds(pl.multiple_of(index * 48, 16), 48)

    def in_plane(p):
        return (p // 8) * 16 + z_hi * 8 + p % 8

    other = me + 8 - 16 * z_hi
    mine = z_hi * 32
    theirs = 32 - mine

    def send_in_plane(base, target, slot, first):
        def one(o, carry):
            p = (p1 + o) % 32
            pltpu.make_async_remote_copy(
                src_ref=send_r.at[rows48(base + p)], dst_ref=target, send_sem=ssem.at[6],
                recv_sem=rsem.at[slot], device_id=(dp, in_plane(p)), device_id_type=MESH,
            ).start()
            return carry

        lax.fori_loop(first, 32, one, 0)

    def send_direct(o, carry):
        p = (p1 + o) % 32
        pltpu.make_async_remote_copy(
            src_ref=send_r.at[rows48(theirs + p)], dst_ref=rows_out.at[rows48(me)], send_sem=ssem.at[6],
            recv_sem=rsem.at[2], device_id=(dp, in_plane(p) + 8 - 16 * z_hi), device_id_type=MESH,
        ).start()
        return carry

    def send_across(first, last):
        def one(o, carry):
            p = (p1 + 64 - o) % 32
            pltpu.make_async_remote_copy(
                src_ref=relay.at[rows48(p)], dst_ref=rows_out.at[rows48(in_plane(p))],
                send_sem=ssem.at[7], recv_sem=rsem.at[2],
                device_id=(dp, other), device_id_type=MESH,
            ).start()
            return carry

        lax.fori_loop(DIRECT + 1 + first, DIRECT + 1 + last, one, 0)

    image_quarter(theirs // 16)
    image_quarter(theirs // 16 + 1)
    send_in_plane(theirs, relay.at[rows48(p1)], 6, DIRECT + 1)
    lax.fori_loop(1, DIRECT + 1, send_direct, 0)
    relay[rows48(p1), :] = send_r[rows48(theirs + p1), :]
    image_quarter(mine // 16)
    image_quarter(mine // 16 + 1)
    own = pltpu.make_async_copy(send_r.at[rows48(mine + p1)], rows_out.at[rows48(me)], lsem.at[14])
    own.start()
    send_in_plane(mine, rows_out.at[rows48(me)], 2, 1)

    arrived(recv_i, 1)
    view = relay.at[pl.ds(0, (31 - DIRECT) * 48)]
    pltpu.make_async_remote_copy(
        src_ref=view, dst_ref=view, send_sem=ssem.at[6], recv_sem=rsem.at[6],
        device_id=(dp, me), device_id_type=MESH,
    ).wait_recv()
    send_across(0, AHEAD)
    by_mode(recv_i)

    def layer(kk, carry):
        here = mode_rows(kk)
        for q in range(2):
            cols = slice(384 * q, 384 * q + 384)
            spec[here, cols] = (dot(latf_v[256 * q:256 * q + 256, :], xt[kk]) * factor).astype(BF)
        pre = dot(spec[here, :], m1[...])
        for q in range(2):
            cols = slice(384 * q, 384 * q + 384)
            kept = (pre[:, cols] + b1_ref[q:q + 1, :]) * relu[here, cols].astype(F32)
            hid[here, cols] = kept.astype(BF)
        return carry

    lax.fori_loop(0, 4, layer, 0)

    lanes = lax.broadcasted_iota(jnp.int32, (96, 384), 1) // 96
    for which, (left, right) in enumerate(((spec, done), (hid, dtwo))):
        acc_a[...] = jnp.zeros_like(acc_a)
        acc_b[...] = jnp.zeros_like(acc_b)
        acc_s[...] = jnp.zeros_like(acc_s)

        def add(kk, carry, left=left, right=right):
            here = mode_rows(kk)
            r = right[here, :]
            acc_a[...] += dot_tn(left[here, 0:384], r)
            acc_b[...] += dot_tn(left[here, 384:768], r)
            acc_s[...] += dot(jnp.ones((8, 256), BF), r)
            return carry

        lax.fori_loop(0, 4, add, 0)
        real = jnp.zeros((96, 384), F32)
        imag = jnp.zeros((96, 384), F32)
        for b in range(4):
            up = slice(96 * b, 96 * b + 96)
            real = jnp.where(lanes == b, acc_a[up, 0:384] + acc_b[up, 384:768], real)
            imag = jnp.where(lanes == b, acc_a[up, 384:768] - acc_b[up, 0:384], imag)
        fold[0:96, 0:384] = real
        fold[0:96, 384:768] = imag
        for r in range(12):
            for c in range(6):
                t = which * 72 + r * 6 + c
                parts[t // 5, t % 5] = fold[8 * r:8 * r + 8, 128 * c:128 * c + 128]
        for c in range(6):
            t = 144 + c
            sums = acc_s[:, 128 * c:128 * c + 128]
            if which == 0:
                parts[t // 5, t % 5] = sums
            else:
                first = lax.broadcasted_iota(jnp.int32, (8, 128), 0) == 0
                parts[t // 5, t % 5] = jnp.where(first, parts[t // 5, t % 5], sums)
    for t in range(150, 160):
        parts[t // 5, t % 5] = jnp.zeros((8, 128), F32)

    def wait_all(ref, count, slot):
        view = ref.at[pl.ds(0, count)]
        pltpu.make_async_remote_copy(
            src_ref=view, dst_ref=view, send_sem=ssem.at[slot], recv_sem=rsem.at[slot],
            device_id=(dp, me), device_id_type=MESH,
        ).wait()

    plane[p1] = parts[p1]

    def scatter(o, carry):
        p = (p1 + o) % 32
        pltpu.make_async_remote_copy(
            src_ref=parts.at[p], dst_ref=plane.at[p1], send_sem=ssem.at[3], recv_sem=rsem.at[3],
            device_id=(dp, in_plane(p)), device_id_type=MESH,
        ).start()
        return carry

    lax.fori_loop(1, 32, scatter, 0)
    wait_all(plane, 31, 3)
    chunk[...] = plane[0]

    def add_plane(p, carry):
        chunk[...] += plane[p]
        return carry

    lax.fori_loop(1, 32, add_plane, 0)
    column[zi] = chunk[...]

    def along_z(o, carry):
        z = (zi + o) % 8
        pltpu.make_async_remote_copy(
            src_ref=chunk, dst_ref=column.at[zi], send_sem=ssem.at[4], recv_sem=rsem.at[4],
            device_id=(z % 4, x * 16 + (z // 4) * 8 + low), device_id_type=MESH,
        ).start()
        return carry

    lax.fori_loop(1, 8, along_z, 0)
    send_across(AHEAD, 32 - DIRECT)
    wait_all(column, 7, 4)
    total = column[0]
    for z in range(1, 8):
        total = total + column[z]
    result[...] = total * norm
    gathered[p1] = result[...]

    def gather(o, carry):
        p = (p1 + o) % 32
        pltpu.make_async_remote_copy(
            src_ref=result, dst_ref=gathered.at[p1], send_sem=ssem.at[5], recv_sem=rsem.at[5],
            device_id=(dp, in_plane(p)), device_id_type=MESH,
        ).start()
        return carry

    lax.fori_loop(1, 32, gather, 0)
    wait_all(gathered, 31, 5)
    grads = pltpu.make_async_copy(gathered, grads_out, lsem.at[15])
    grads.start()

    grads.wait()
    own.wait()
    arrived(rows_out, 2)
    for slot, count in ((0, 63), (1, 63), (6, 62), (7, 32 - DIRECT)):
        view = recv_c.at[pl.ds(0, count * 48)]
        pltpu.make_async_remote_copy(
            src_ref=view, dst_ref=view, send_sem=ssem.at[slot], recv_sem=rsem.at[slot],
            device_id=(dp, me), device_id_type=MESH,
        ).wait_send()


def last_kernel(
    factor, rows_hbm, cot_hbm, table_hbm, grads_hbm, out_hbm, w1_hbm, b1_hbm, w2_hbm, b2_hbm,
    rows_v, cot_v, table_v, grads_v, out_v, w1_v, b1_v, w2_v, b2_v, rsem, csem, tsem, osem, gsem,
):
    table_load = [
        pltpu.make_async_copy(table_hbm.at[pl.ds(256 * m, 256)], table_v.at[pl.ds(256 * m, 256)], tsem.at[m])
        for m in range(3)
    ]
    rows_load = [
        [
            pltpu.make_async_copy(
                rows_hbm.at[pl.ds(32 * s, 32), hp], rows_v.at[hp, pl.ds(32 * s, 32)], rsem.at[hp, s]
            )
            for s in range(2)
        ]
        for hp in range(3)
    ]
    cot_load = [pltpu.make_async_copy(cot_hbm.at[h], cot_v.at[h], csem.at[h]) for h in range(6)]
    grads_load = pltpu.make_async_copy(grads_hbm, grads_v, gsem.at[0])
    for load in rows_load[0]:
        load.start()
    for load in table_load:
        load.start()
    for hp in range(3):
        cot_load[2 * hp].start()
        cot_load[2 * hp + 1].start()
        if hp == 0:
            grads_load.start()
        if hp < 2:
            for load in rows_load[hp + 1]:
                load.start()

    stores = [pltpu.make_async_copy(out_v.at[h], out_hbm.at[h], osem.at[h]) for h in range(6)]
    small = [
        pltpu.make_async_copy(here, there, gsem.at[1 + i])
        for i, (here, there) in enumerate(((w1_v, w1_hbm), (b1_v, b1_hbm), (w2_v, w2_hbm), (b2_v, b2_hbm)))
    ]

    def tiles(first):
        return jnp.concatenate([grads_v[t // 5, t % 5] for t in range(first, first + 6)], axis=1)

    for hp in range(3):
        for load in rows_load[hp]:
            load.wait()
        rows = rows_v[hp].astype(F32)
        for half in range(2):
            image = rows[:, 8 * half:8 * half + 8, :].reshape(512, 384).astype(BF)
            if half == 0:
                first = image
        for h in (2 * hp, 2 * hp + 1):
            cot_load[h].wait()
        pair = jnp.concatenate([first, image], axis=1)
        for m in range(3):
            if hp == 0:
                table_load[m].wait()
            part = slice(256 * m, 256 * m + 256)
            field = dot(table_v[part, :], pair) * factor
            for half in range(2):
                h = 2 * hp + half
                cols = slice(384 * half, 384 * half + 384)
                out_v[h, part, :] = (cot_v[h, part, :].astype(F32) + field[:, cols]).astype(BF)
        for h in (2 * hp, 2 * hp + 1):
            stores[h].start()
        if hp == 0:
            grads_load.wait()
            for which, out in enumerate((w1_v, w2_v)):
                for r in range(12):
                    line = tiles(which * 72 + r * 6)
                    for q in range(2):
                        for b in range(4):
                            start = q * 384 + b * 96
                            out[q, b, 8 * r:8 * r + 8, :] = line[:, start:start + 96]
            line = tiles(144)
            for which, out in enumerate((b1_v, b2_v)):
                for q in range(2):
                    out[q:q + 1, :] = line[which:which + 1, 384 * q:384 * q + 384]
            for copy in small:
                copy.start()
    for copy in small + stores:
        copy.wait()


def last_call(factor, rows, cot, table, grads):
    any_spec = pl.BlockSpec(memory_space=pl.ANY)
    small = [(2, 4, 96, 96), (2, 384)] * 2
    return pl.pallas_call(
        functools.partial(last_kernel, factor),
        out_shape=(jax.ShapeDtypeStruct((6, 768, 384), BF),) + tuple(jax.ShapeDtypeStruct(s, F32) for s in small),
        in_specs=[any_spec] * 4,
        out_specs=(any_spec,) * 5,
        scratch_shapes=[
            pltpu.VMEM((3, 64, 16, 384), BF), pltpu.VMEM((6, 768, 384), BF), pltpu.VMEM((768, 512), BF),
            pltpu.VMEM((32, 5, 8, 128), F32), pltpu.VMEM((6, 768, 384), BF),
        ] + [pltpu.VMEM(s, F32) for s in small] + [
            pltpu.SemaphoreType.DMA((3, 2)), pltpu.SemaphoreType.DMA((6,)), pltpu.SemaphoreType.DMA((3,)),
            pltpu.SemaphoreType.DMA((6,)), pltpu.SemaphoreType.DMA((5,)),
        ],
        compiler_params=pltpu.CompilerParams(vmem_limit_bytes=62 * MIB),
        name="field",
    )(rows, cot, table, grads)


def local(inputs, cotangent, masks, w_first, b_first, w_second):
    factor = 1.0 / math.sqrt(384 * 768)
    norm = 1.0 / math.sqrt(4 * 256 * 256)
    lon, lon_t = lon_tables(256, 768, 64)
    lat_f, lat_b = lat_tables(256, 384)
    perm_f, perm_b = permutation(32, 4)
    cot = cotangent[0]
    any_spec = pl.BlockSpec(memory_space=pl.ANY)
    wide = (1024, 768)
    rows, grads = pl.pallas_call(
        functools.partial(main_kernel, factor, norm),
        out_shape=(
            jax.ShapeDtypeStruct((3072, 384), BF),
            jax.ShapeDtypeStruct((32, 5, 8, 128), F32),
        ),
        in_specs=[any_spec] * 11,
        out_specs=(any_spec, any_spec),
        scratch_shapes=[
            pltpu.VMEM((6, 768, 384), BF), pltpu.VMEM((6, 768, 384), BF),
            pltpu.VMEM((256, 4, 384), jnp.int32),
            pltpu.VMEM((512, 768), BF), pltpu.VMEM((512, 768), BF), pltpu.VMEM((768, 512), BF),
            pltpu.VMEM((256, 256), BF), pltpu.VMEM((256, 256), BF),
            pltpu.VMEM((2, 4, 96, 96), BF), pltpu.VMEM((2, 384), F32), pltpu.VMEM((2, 4, 96, 96), BF),
            pltpu.VMEM((3, 64, 16, 384), BF), pltpu.VMEM((3, 64, 16, 384), BF), pltpu.VMEM((3072, 384), BF), pltpu.VMEM((1536, 384), BF),
            pltpu.VMEM((3072, 384), BF), pltpu.VMEM((3072, 384), BF),
            pltpu.VMEM((4, 768, 384), BF),
            pltpu.VMEM(wide, BF), pltpu.VMEM(wide, BF), pltpu.VMEM(wide, BF), pltpu.VMEM(wide, BF),
            pltpu.VMEM((4, 512, 384), BF),
            pltpu.VMEM(wide, BF), pltpu.VMEM(wide, BF),
            pltpu.VMEM((768, 768), BF), pltpu.VMEM((768, 768), BF), pltpu.VMEM((768, 768), BF),
            pltpu.VMEM((384, 768), F32), pltpu.VMEM((384, 768), F32), pltpu.VMEM((8, 768), F32),
            pltpu.VMEM((96, 768), F32),
            pltpu.VMEM((32, 5, 8, 128), F32), pltpu.VMEM((32, 5, 8, 128), F32), pltpu.VMEM((32, 5, 8, 128), F32),
            pltpu.VMEM((8, 5, 8, 128), F32), pltpu.VMEM((5, 8, 128), F32), pltpu.VMEM((5, 8, 128), F32),
            pltpu.SemaphoreType.DMA((16,)), pltpu.SemaphoreType.DMA((8,)), pltpu.SemaphoreType.DMA((7,)),
        ],
        compiler_params=pltpu.CompilerParams(
            collective_id=0, has_side_effects=True, vmem_limit_bytes=62 * MIB
        ),
        name="exchange",
    )(cot, inputs[0], masks[0], lon, lat_f, lat_b, perm_f, perm_b, w_first, b_first, w_second)
    field, w1, b1, w2, b2 = last_call(factor, rows.reshape(64, 3, 16, 384), cot, lon_t, grads)
    return field[None], w1, b1, w2, b2


def solution(mesh):
    placed = (
        P("dp", "sp", None, None),
        P("dp", "sp", None, None),
        P("dp", None, "sp", None),
        P(),
        P(),
        P(),
    )
    return jax.shard_map(
        local,
        mesh=mesh,
        in_specs=placed,
        out_specs=(P("dp", "sp", None, None), P(), P(), P(), P()),
        check_vma=False,
    )
```
